32 devices in a mesh: dp: 16 (over z, y, x), tensor: 2 (over core).
Axes of the slice: x: 2, y: 2, z: 4, core: 2. Of those that a mesh axis runs over, the one named last changes fastest.
Arguments:
- tokens: bfloat16 [16384, 768], P(('dp', 'tensor')), may hold values from -6 to 6
- lengths: int32 [48], replicated, may hold values from 32 to 1024, as said below
- owners: int32 [48], replicated, may hold values from 0 to 15
- gain_first: bfloat16 [768], replicated, may hold values from 0.5 to 1.5
- shift_first: bfloat16 [768], replicated, may hold values from -1.1953125 to 1.1953125
- query_weight: bfloat16 [768, 768], P(None, 'tensor'), may hold values from -0.21875 to 0.21875
- key_weight: bfloat16 [768, 768], P(None, 'tensor'), may hold values from -0.21875 to 0.21875
- value_weight: bfloat16 [768, 768], P(None, 'tensor'), may hold values from -0.21875 to 0.21875
- query_bias: bfloat16 [768], P('tensor'), may hold values from -1.1953125 to 1.1953125
- value_bias: bfloat16 [768], P('tensor'), may hold values from -1.1953125 to 1.1953125
- output_weight: bfloat16 [768, 768], P('tensor'), may hold values from -2.5 to 2.5
- output_bias: bfloat16 [768], replicated, may hold values from -1.1953125 to 1.1953125
- gain_second: bfloat16 [768], replicated, may hold values from 0.5 to 1.5
- shift_second: bfloat16 [768], replicated, may hold values from -1.1953125 to 1.1953125
- expand_weight: bfloat16 [768, 3072], P(None, 'tensor'), may hold values from -0.21875 to 0.21875
- expand_bias: bfloat16 [3072], P('tensor'), may hold values from -1.1953125 to 1.1953125
- contract_weight: bfloat16 [3072, 768], P('tensor'), may hold values from -0.15625 to 0.15625
- contract_bias: bfloat16 [768], replicated, may hold values from -1.1953125 to 1.1953125
- cotangent: bfloat16 [16384, 768], P(('dp', 'tensor')), may hold values from -6 to 6
Outputs:
- result: bfloat16 [16384, 768], P(('dp', 'tensor'))
- tokens_grad: bfloat16 [16384, 768], P(('dp', 'tensor'))
- gain_first_grad: float32 [768], replicated
- shift_first_grad: float32 [768], replicated
- query_weight_grad: float32 [768, 768], P(None, 'tensor')
- key_weight_grad: float32 [768, 768], P(None, 'tensor')
- value_weight_grad: float32 [768, 768], P(None, 'tensor')
- query_bias_grad: float32 [768], P('tensor')
- value_bias_grad: float32 [768], P('tensor')
- output_weight_grad: float32 [768, 768], P('tensor')
- output_bias_grad: float32 [768], replicated
- gain_second_grad: float32 [768], replicated
- shift_second_grad: float32 [768], replicated
- expand_weight_grad: float32 [768, 3072], P(None, 'tensor')
- expand_bias_grad: float32 [3072], P('tensor')
- contract_weight_grad: float32 [3072, 768], P('tensor')
- contract_bias_grad: float32 [768], replicated
The draws below stay inside these ranges and needn't reach their ends.
Inputs may be any that keep to these rules, and one draw needn't show every extreme that they name: Sequence i has lengths[i] tokens and lies in data group owners[i]; the sequences of a group follow one another in order of their index from the group's first row, and rows after them belong to no sequence. The lengths of a group sum to at most 1024; every group holds at least one sequence; in every draw one group holds a single sequence of exactly 1024 tokens.
All inputs are finite; a program needn't handle non-finite values.
Results may differ from the reference program's by a relative error of at most 0.012.
Values may be sent and summed in bfloat16 or wider, within the bound.
A program may use at most 128 MiB of HBM per device.

```python
import jax
import jax.numpy as jnp
from jax import lax

D = 768
HEADS = 12
HD = 64
FF = 3072
CAP = 1024
NSEQ = 48
TOKENS = 16384
N_DP = 16


def layout(key):
    groups = TOKENS // CAP
    slots = 4 * groups
    key_length, key_full, key_pick, key_order = jax.random.split(key, 4)
    pattern = jnp.array([CAP // 2, CAP // 4, CAP // 8, CAP // 8], dtype=jnp.int32)
    limits = jnp.tile(pattern, groups)
    drawn = jax.random.randint(key_length, (slots,), limits // 4, limits + 1, dtype=jnp.int32)
    chosen_group = jax.random.randint(key_full, (), 0, groups, dtype=jnp.int32)
    index = jnp.arange(slots, dtype=jnp.int32)
    slot_owner = index // 4
    leading = index % 4 == 0
    drawn = jnp.where(leading & (slot_owner == chosen_group), CAP, drawn)
    priority = jax.random.permutation(key_pick, slots).astype(jnp.int32)
    excluded = jnp.logical_not(leading) & (slot_owner == chosen_group)
    ranking = jnp.where(leading, -1 - index, jnp.where(excluded, slots + index, priority))
    picked = jnp.argsort(ranking, stable=True)[:NSEQ]
    shuffle = jax.random.permutation(key_order, NSEQ)
    picked = picked[shuffle]
    return (drawn[picked], slot_owner[picked])


def draw_lengths(key, part):
    return layout(key)[0]


def draw_owners(key, part):
    return layout(key)[1]


def steps_of(key, shape, pieces, least, largest):
    factor_of, own = 1.0, jax.random.fold_in(key, 6)
    for position, blocks in pieces:
        heights = jnp.exp(jax.random.uniform(jax.random.fold_in(own, position), (blocks,), jnp.float32, least / len(pieces), largest / len(pieces)))
        factor_of = factor_of * jnp.repeat(heights, shape[position] // blocks).reshape([-1 if axis == position else 1 for axis in range(len(shape))])
    return factor_of


def gaussian(own_key, extent, spread, bound, pieces=(), kind=jnp.bfloat16):
    values = jax.random.normal(own_key, extent, jnp.float32) * spread
    if len(pieces) > 0:
        values = steps_of(own_key, extent, pieces, -0.22, 0.18) * values
    return jnp.clip(values, min=-bound, max=bound).astype(kind)


def setup_inputs(seed: int = 0) -> dict:
    key_of = jax.random.split(jax.random.key(seed), 20)
    tokens = gaussian(key_of[0], (TOKENS, D), 1.0, 6.0, ((0, 32),))
    lengths = draw_lengths(jax.random.fold_in(key_of[19], 71), 0)
    owners = draw_owners(jax.random.fold_in(key_of[19], 71), 0)
    gain_first = jnp.clip(1.0 + 0.1 * jax.random.normal(key_of[3], (D,), jnp.float32), 0.5, 1.5).astype(jnp.bfloat16)
    shift_first = gaussian(key_of[4], (D,), 0.3, 1.1953125)
    query_weight = gaussian(key_of[5], (D, D), D ** -0.5, 0.21875, ((1, 2),))
    key_weight = gaussian(key_of[6], (D, D), D ** -0.5, 0.21875, ((1, 2),))
    value_weight = gaussian(key_of[7], (D, D), D ** -0.5, 0.21875, ((1, 2),))
    query_bias = gaussian(key_of[8], (D,), 0.3, 1.1953125, ((0, 2),))
    value_bias = gaussian(key_of[9], (D,), 0.3, 1.1953125, ((0, 2),))
    output_weight = gaussian(key_of[10], (D, D), (max(D // 128, 2)) ** -0.5, 2.5, ((0, 2),))
    output_bias = gaussian(key_of[11], (D,), 0.3, 1.1953125)
    gain_second = jnp.clip(1.0 + 0.1 * jax.random.normal(key_of[12], (D,), jnp.float32), 0.5, 1.5).astype(jnp.bfloat16)
    shift_second = gaussian(key_of[13], (D,), 0.3, 1.1953125)
    expand_weight = gaussian(key_of[14], (D, FF), D ** -0.5, 0.21875, ((1, 2),))
    expand_bias = gaussian(key_of[15], (FF,), 0.3, 1.1953125, ((0, 2),))
    contract_weight = gaussian(key_of[16], (FF, D), (FF // 2) ** -0.5, 0.15625, ((0, 2),))
    contract_bias = gaussian(key_of[17], (D,), 0.3, 1.1953125)
    cotangent = gaussian(key_of[18], (TOKENS, D), 1.0, 6.0, ((0, 32),))
    return dict(tokens=tokens, lengths=lengths, owners=owners, gain_first=gain_first, shift_first=shift_first, query_weight=query_weight, key_weight=key_weight, value_weight=value_weight, query_bias=query_bias, value_bias=value_bias, output_weight=output_weight, output_bias=output_bias, gain_second=gain_second, shift_second=shift_second, expand_weight=expand_weight, expand_bias=expand_bias, contract_weight=contract_weight, contract_bias=contract_bias, cotangent=cotangent)


@jax.custom_vjp
def low(v):
    return lax.optimization_barrier(v.astype(jnp.bfloat16)).astype(jnp.float32)

@jax.custom_vjp
def low_back(v):
    return v

def low_keep(v):
    return (low(v), None)

def low_pass(kept, grad):
    return (grad,)

def back_keep(v):
    return (v, None)

def back_low(kept, grad):
    return (low(grad),)
low.defvjp(low_keep, low_pass)
low_back.defvjp(back_keep, back_low)
epsilon = 1e-05

def layer_norm(values, gain, shift):
    average = lax.optimization_barrier(jnp.mean(values, axis=-1, keepdims=True))
    centred = values - average
    variance = lax.optimization_barrier(jnp.mean(centred * centred, axis=-1, keepdims=True))
    return centred * lax.rsqrt(variance + epsilon) * gain + shift

def matmul(left, right):
    return jnp.dot(left, right, precision=lax.Precision.HIGHEST, preferred_element_type=jnp.float32)

def row_segments(lengths, owners, group, total_rows):
    count = lengths.shape[0]
    index = jnp.arange(count, dtype=jnp.int32)
    same = owners[None, :] == owners[:, None]
    earlier = index[None, :] < index[:, None]
    starts = lax.optimization_barrier(jnp.sum(jnp.where(same & earlier, lengths[None, :], 0), axis=1, dtype=jnp.int32))
    positions = jnp.arange(total_rows, dtype=jnp.int32)[:, None]
    inside = (owners[None, :] == group) & (positions >= starts[None, :]) & (positions < starts[None, :] + lengths[None, :])
    return lax.optimization_barrier(jnp.sum(jnp.where(inside, index[None, :] + 1, 0), axis=1, dtype=jnp.int32))

def attend(query, keys, values, segments):
    block = min(512, CAP)
    count = CAP // block
    positions = jnp.arange(CAP, dtype=jnp.int32)
    scale = HD ** (-0.5)

    def one(index):
        start = index * block
        query_block = lax.dynamic_slice_in_dim(query, start, block, 0)
        segment_block = lax.dynamic_slice_in_dim(segments, start, block, 0)
        rows_here = start + jnp.arange(block, dtype=jnp.int32)
        allowed = (segment_block[:, None] == segments[None, :]) & (positions[None, :] <= rows_here[:, None])
        scores = low_back(jnp.einsum('qhd,khd->hqk', query_block, keys, precision=lax.Precision.HIGHEST) * scale)
        scores = jnp.where(allowed[None], scores, -1e+30)
        top = lax.optimization_barrier(jnp.max(scores, axis=-1, keepdims=True))
        powers = jnp.exp(scores - top)
        probs = low(powers / lax.optimization_barrier(jnp.sum(powers, axis=-1, keepdims=True)))
        return jnp.einsum('hqk,khd->qhd', probs, values, precision=lax.Precision.HIGHEST)
    mixed = lax.map(jax.checkpoint(one), jnp.arange(count, dtype=jnp.int32))
    return mixed.reshape(CAP, HEADS * HD)

def block_forward(inputs, live, segments, params):
    gain_first, shift_first, query_weight, key_weight, value_weight, query_bias, value_bias, output_weight, output_bias, gain_second, shift_second, expand_weight, expand_bias, contract_weight, contract_bias = params
    split = (CAP, HEADS, HD)
    normed = low(layer_norm(inputs, gain_first, shift_first))
    query = low(low_back(matmul(normed, query_weight) + query_bias)).reshape(split)
    keys = low(low_back(matmul(normed, key_weight))).reshape(split)
    values = low(low_back(matmul(normed, value_weight) + value_bias)).reshape(split)
    mixed = low(low_back(attend(query, keys, values, segments)))
    hidden = inputs + live * low_back(matmul(mixed, output_weight) + output_bias)
    middle = low(layer_norm(hidden, gain_second, shift_second))
    before = low_back(matmul(middle, expand_weight) + expand_bias)
    active = low(jax.nn.gelu(before, approximate=True))
    return hidden + live * low_back(matmul(active, contract_weight) + contract_bias)

def reference(tokens, lengths, owners, gain_first, shift_first, query_weight, key_weight, value_weight, query_bias, value_bias, output_weight, output_bias, gain_second, shift_second, expand_weight, expand_bias, contract_weight, contract_bias, cotangent):
    params = tuple((item.astype(jnp.float32) for item in (gain_first, shift_first, query_weight, key_weight, value_weight, query_bias, value_bias, output_weight, output_bias, gain_second, shift_second, expand_weight, expand_bias, contract_weight, contract_bias)))
    inputs = tokens.astype(jnp.float32).reshape(N_DP, CAP, D)
    upstream = cotangent.astype(jnp.float32).reshape(N_DP, CAP, D)

    def step(totals, items):
        group_inputs, group_upstream, group = items
        segments = row_segments(lengths, owners, group, CAP)
        live = (segments > 0).astype(jnp.float32)[:, None]

        def forward(values, *weights):
            return block_forward(values, live, segments, weights)
        output, pull = jax.vjp(forward, group_inputs, *params)
        grads = pull(group_upstream)
        totals = tuple((left + right for left, right in zip(totals, grads[1:])))
        return (totals, (output.astype(jnp.bfloat16), grads[0].astype(jnp.bfloat16)))
    zeros = tuple((jnp.zeros_like(item) for item in params))
    totals, (result, tokens_grad) = lax.scan(step, zeros, (inputs, upstream, jnp.arange(N_DP, dtype=jnp.int32)))
    return (result.reshape(TOKENS, D), tokens_grad.reshape(TOKENS, D), totals[0], totals[1], totals[2], totals[3], totals[4], totals[5], totals[6], totals[7], totals[8], totals[9], totals[10], totals[11], totals[12], totals[13], totals[14])
```

```python
import functools

import jax
import jax.numpy as jnp
from jax import lax
from jax.experimental import pallas as pl
from jax.experimental.pallas import tpu as pltpu
from jax.sharding import PartitionSpec as P

HD = 64


epsilon = 1e-05


def layer_norm(values, gain, shift):
    average = jnp.mean(values, axis=-1, keepdims=True)
    centred = values - average
    variance = jnp.mean(centred * centred, axis=-1, keepdims=True)
    return centred * lax.rsqrt(variance + epsilon) * gain + shift


def gelu_tanh(values):
    return jax.nn.gelu(values, approximate=True)


def row_segments(lengths, owners, group, total_rows):
    count = lengths.shape[0]
    index = jnp.arange(count, dtype=jnp.int32)
    same = owners[None, :] == owners[:, None]
    earlier = index[None, :] < index[:, None]
    starts = jnp.sum(jnp.where(same & earlier, lengths[None, :], 0), axis=1, dtype=jnp.int32)
    positions = jnp.arange(total_rows, dtype=jnp.int32)[:, None]
    inside = (
        (owners[None, :] == group)
        & (positions >= starts[None, :])
        & (positions < starts[None, :] + lengths[None, :])
    )
    segments = jnp.sum(jnp.where(inside, index[None, :] + 1, 0), axis=1, dtype=jnp.int32)
    used = jnp.sum(jnp.where(owners == group, lengths, 0), dtype=jnp.int32)
    first = jnp.sum(jnp.where(inside, starts[None, :], 0), axis=1, dtype=jnp.int32)
    return segments, jnp.where(segments > 0, first, used)


def rows_product(left, right):
    return lax.dot_general(
        left, right, (((0,), (0,)), ((), ())), preferred_element_type=jnp.float32
    )


def transposed_product(left, right):
    return lax.dot_general(
        left, right, (((1,), (1,)), ((), ())), preferred_element_type=jnp.float32
    )


QB = 256
MASKED = -1e30


def heads_dot(left, right, left_dim, right_dim):
    return lax.dot_general(
        left, right, (((left_dim,), (right_dim,)), ((), ())), preferred_element_type=jnp.float32
    )


def fill_mask(first_ref, mask_ref):
    total = mask_ref.shape[0]
    for start in range(0, total, QB):
        rows = start + lax.broadcasted_iota(jnp.int32, (QB, total), 0)
        columns = lax.broadcasted_iota(jnp.int32, (QB, total), 1)
        allowed = (columns >= first_ref[start : start + QB, :]) & (columns <= rows)
        mask_ref[start : start + QB, :] = jnp.where(allowed, 0.0, MASKED)


def forward_kernel(first_ref, query_ref, keys_ref, values_ref, mixed_ref, log_ref, mask_ref):
    @pl.when(pl.program_id(0) == 0)
    def _():
        fill_mask(first_ref, mask_ref)

    total = query_ref.shape[0]
    for start in range(0, total, QB):
        stop = start + QB
        outs, logs = [], []
        for h in range(2):
            lanes = slice(h * HD, (h + 1) * HD)
            scores = heads_dot(query_ref[start:stop, lanes], keys_ref[:stop, lanes], 1, 1)
            scores = scores + mask_ref[start:stop, :stop]
            top = jnp.max(scores, axis=-1, keepdims=True)
            powers = jnp.exp(scores - top)
            sums = jnp.sum(powers, axis=-1, keepdims=True)
            probs = (powers * (1.0 / sums)).astype(jnp.bfloat16)
            outs.append(heads_dot(probs, values_ref[:stop, lanes], 1, 0))
            logs.append(jnp.broadcast_to(top + jnp.log(sums), (QB, HD)))
        mixed_ref[start:stop, :] = jnp.concatenate(outs, axis=1).astype(jnp.bfloat16)
        log_ref[start:stop, :] = jnp.concatenate(logs, axis=1)


def backward_kernel(
    first_ref, query_ref, keys_ref, values_ref, log_ref, grad_ref,
    grad_query_ref, grad_keys_ref, grad_values_ref, mask_ref, keys_sum, values_sum,
):
    @pl.when(pl.program_id(0) == 0)
    def _():
        fill_mask(first_ref, mask_ref)

    total = query_ref.shape[0]
    for start in range(total - QB, -1, -QB):
        stop = start + QB
        parts = ([], [], [])
        for h in range(2):
            lanes = slice(h * HD, (h + 1) * HD)
            query = query_ref[start:stop, lanes]
            grad = grad_ref[start:stop, lanes]
            keys = keys_ref[:stop, lanes]
            scores = heads_dot(query, keys, 1, 1) + mask_ref[start:stop, :stop]
            probs = jnp.exp(scores - log_ref[start:stop, h * HD : h * HD + 1])
            grad_probs = heads_dot(grad, values_ref[:stop, lanes], 1, 1)
            inner = jnp.sum(probs * grad_probs, axis=-1, keepdims=True)
            grad_scores = (probs * (grad_probs - inner)).astype(jnp.bfloat16)
            parts[0].append(heads_dot(grad_scores, keys, 1, 0))
            parts[1].append(heads_dot(grad_scores, query, 0, 0))
            parts[2].append(heads_dot(probs.astype(jnp.bfloat16), grad, 0, 0))
        grad_query_ref[start:stop, :] = (
            jnp.concatenate(parts[0], axis=1) * (HD ** (-0.5))
        ).astype(jnp.bfloat16)
        for sums, part in ((keys_sum, parts[1]), (values_sum, parts[2])):
            part = jnp.concatenate(part, axis=1)
            if stop == total:
                sums[...] = part
            else:
                sums[:stop, :] += part
    grad_keys_ref[...] = keys_sum[...].astype(jnp.bfloat16)
    grad_values_ref[...] = values_sum[...].astype(jnp.bfloat16)


def attention_call(kernel, out_types, scratch, flops, name, first, *operands):
    rows, width = operands[0].shape
    pair = pl.BlockSpec((rows, 2 * HD), lambda i: (0, i))
    return pl.pallas_call(
        kernel,
        grid=(width // (2 * HD),),
        in_specs=[pl.BlockSpec((rows, 1), lambda i: (0, 0))] + [pair] * len(operands),
        out_specs=[pair] * len(out_types),
        out_shape=[jax.ShapeDtypeStruct((rows, width), kind) for kind in out_types],
        scratch_shapes=[pltpu.VMEM((rows, rows), jnp.float32)]
        + [pltpu.VMEM((rows, 2 * HD), jnp.float32)] * scratch,
        compiler_params=pltpu.CompilerParams(vmem_limit_bytes=40 * 1024 * 1024),
        cost_estimate=pl.CostEstimate(
            flops=flops, bytes_accessed=8 * rows * width * 2, transcendentals=rows * rows * 4
        ),
        name=name,
    )(first, *operands)


def swap(values):
    return lax.ppermute(values, "tensor", [(0, 1), (1, 0)])


def sum_kernel(groups, orders, chains, count, *refs):
    inputs, outputs = refs[:count], refs[count : 2 * count]
    works, arrived = refs[2 * count : 3 * count], refs[3 * count : 4 * count]
    send_sem, recv_sem = refs[4 * count :]
    group = lax.axis_index("dp")
    steps = len(orders[0])
    digit = [(group // (1 << bit)) % 2 for bit in range(steps)]
    partner = [group + (1 - 2 * digit[bit]) * (1 << bit) for bit in range(steps)]

    barrier = pltpu.get_barrier_semaphore()
    for bit in range(steps):
        pl.semaphore_signal(
            barrier, inc=1, device_id={"dp": partner[bit]}, device_id_type=pl.DeviceIdType.MESH
        )
    pl.semaphore_wait(barrier, steps)

    def copy(chain, step, bit, source, target):
        slot = chain * 2 * steps + step
        made = pltpu.make_async_remote_copy(
            src_ref=source,
            dst_ref=target,
            send_sem=send_sem.at[slot],
            recv_sem=recv_sem.at[slot],
            device_id={"dp": partner[bit]},
            device_id_type=pl.DeviceIdType.MESH,
        )
        made.start()
        return made

    def rows_at(start, size):
        return pl.ds(pl.multiple_of(start, 16), size)

    offsets = [[0] for _ in chains]
    pending = [None for _ in chains]
    started = []

    def scatter_start(c, step):
        array, low, high, kind = chains[c]
        rows = inputs[array].shape[0]
        half = rows >> (step + 1)
        bit = orders[kind][step]
        source = inputs[array] if step == 0 else works[array]
        sent = offsets[c][-1] + (1 - digit[bit]) * half
        pending[c] = copy(
            c, step, bit,
            source.at[rows_at(sent, half), low:high],
            arrived[array].at[rows - 2 * half : rows - half, low:high],
        )
        started.append(pending[c])
        offsets[c].append(offsets[c][-1] + digit[bit] * half)

    def scatter_add(c, step):
        array, low, high, kind = chains[c]
        rows = inputs[array].shape[0]
        half = rows >> (step + 1)
        kept = offsets[c][-1]
        pending[c].wait_recv()
        tile = 48 if half % 48 == 0 else 16
        source = inputs[array] if step == 0 else works[array]
        target = outputs[array] if step == steps - 1 else works[array]

        def add(i, carry):
            here = rows_at(kept + i * tile, tile)
            there = rows_at(rows - 2 * half + i * tile, tile)
            total = source[here, low:high].astype(jnp.float32) + arrived[array][
                there, low:high
            ].astype(jnp.float32)
            target[here, low:high] = total.astype(jnp.bfloat16)
            return carry

        lax.fori_loop(0, half // tile, add, 0)

    def gather_start(c, step):
        array, low, high, kind = chains[c]
        size = inputs[array].shape[0] >> step
        block = outputs[array].at[rows_at(offsets[c][step], size), low:high]
        pending[c] = copy(c, 2 * steps - step, orders[kind][step - 1], block, block)
        started.append(pending[c])

    every = range(len(chains))
    for c in every:
        scatter_start(c, 0)
    for step in range(steps):
        for c in every:
            scatter_add(c, step)
            if step < steps - 1:
                scatter_start(c, step + 1)
            else:
                gather_start(c, steps)
    for step in range(steps - 1, 0, -1):
        for c in every:
            pending[c].wait_recv()
            gather_start(c, step)
    for c in every:
        pending[c].wait_recv()
    for made in started:
        made.wait_send()


def sum_over_groups(arrays, groups):
    if any(array.shape[0] % (16 * groups) for array in arrays):
        return lax.psum(tuple(arrays), "dp")
    bits = list(range(groups.bit_length() - 1))
    orders = (bits, bits[1:2] + bits[:1] + bits[2:], bits[2:] + bits[:2])
    chains = []
    for index, array in enumerate(arrays):
        width = array.shape[1]
        if index == 0:
            cuts = [(0, width // 2, 0), (width // 2, width, 1)]
        elif index in (1, 2):
            third = width // 3
            cuts = [(i * third, (i + 1) * third, i) for i in range(3)]
        else:
            cuts = [(0, width, index - 3)]
        chains += [(index,) + cut for cut in cuts]
    count = len(arrays)
    slots = len(chains) * 2 * len(bits)
    shapes = [jax.ShapeDtypeStruct(array.shape, array.dtype) for array in arrays]
    buffers = [pltpu.VMEM(array.shape, array.dtype) for array in arrays]
    vmem = pl.BlockSpec(memory_space=pltpu.VMEM)
    return pl.pallas_call(
        functools.partial(sum_kernel, groups, orders, chains, count),
        out_shape=shapes,
        in_specs=[vmem] * count,
        out_specs=[vmem] * count,
        scratch_shapes=buffers
        + buffers
        + [pltpu.SemaphoreType.DMA((slots,)), pltpu.SemaphoreType.DMA((slots,))],
        compiler_params=pltpu.CompilerParams(
            collective_id=0, has_side_effects=True, vmem_limit_bytes=48 * 1024 * 1024
        ),
        name="sum_over_groups",
    )(*arrays)


def on_device(
    tokens,
    lengths,
    owners,
    gain_first,
    shift_first,
    query_weight,
    key_weight,
    value_weight,
    query_bias,
    value_bias,
    output_weight,
    output_bias,
    gain_second,
    shift_second,
    expand_weight,
    expand_bias,
    contract_weight,
    contract_bias,
    cotangent,
):
    own_rows = tokens.shape[0]
    group = lax.axis_index("dp")
    side = lax.axis_index("tensor")
    first_row = side * own_rows
    other_row = (1 - side) * own_rows

    def in_order(own, other):
        return jnp.concatenate(
            [jnp.where(side == 0, own, other), jnp.where(side == 0, other, own)], axis=0
        )

    def halves(values):
        return (
            lax.dynamic_slice_in_dim(values, first_row, own_rows, 0),
            lax.dynamic_slice_in_dim(values, other_row, own_rows, 0),
        )

    segments, firsts = row_segments(lengths, owners, group, 2 * own_rows)
    firsts = firsts[:, None]
    own_segments = lax.dynamic_slice_in_dim(segments, first_row, own_rows, 0)
    live = (own_segments > 0).astype(jnp.float32)[:, None]
    scale = HD ** (-0.5)
    width = query_weight.shape[1]
    upstream = cotangent.astype(jnp.float32)
    own_two = (live * upstream).astype(jnp.bfloat16)
    inputs = tokens.astype(jnp.float32)
    normed_value, pull_first = jax.vjp(
        layer_norm, inputs, gain_first.astype(jnp.float32), shift_first.astype(jnp.float32)
    )
    own_normed = normed_value.astype(jnp.bfloat16)
    normed = in_order(own_normed, swap(own_normed))
    grad_two = jnp.concatenate([own_two, swap(own_two)], axis=0)
    query = (
        jnp.dot(normed, query_weight, preferred_element_type=jnp.float32)
        + query_bias.astype(jnp.float32)
    ).astype(jnp.bfloat16) * jnp.bfloat16(scale)
    keys = jnp.dot(normed, key_weight, preferred_element_type=jnp.float32).astype(jnp.bfloat16)
    values = (
        jnp.dot(normed, value_weight, preferred_element_type=jnp.float32)
        + value_bias.astype(jnp.float32)
    ).astype(jnp.bfloat16)
    pairs = 2 * own_rows * 2 * own_rows * width
    mixed, logs = attention_call(
        forward_kernel, (jnp.bfloat16, jnp.float32), 0, 3 * pairs, "attend",
        firsts, query, keys, values,
    )

    def summed(product, values, send_type=jnp.bfloat16):
        own, other = values
        received = swap(product(other).astype(send_type))
        return product(own) + received.astype(jnp.float32)

    branch = summed(
        lambda rows: jnp.dot(rows, output_weight, preferred_element_type=jnp.float32),
        halves(mixed),
    ) + output_bias.astype(jnp.float32)
    hidden = inputs + live * branch
    middle_value, pull_second = jax.vjp(
        layer_norm, hidden, gain_second.astype(jnp.float32), shift_second.astype(jnp.float32)
    )
    own_middle = middle_value.astype(jnp.bfloat16)
    middle = jnp.concatenate([own_middle, swap(own_middle)], axis=0)
    before = jnp.dot(
        middle, expand_weight, preferred_element_type=jnp.float32
    ) + expand_bias.astype(jnp.float32)
    active_value, pull_active = jax.vjp(gelu_tanh, before)
    active = active_value.astype(jnp.bfloat16)
    contract_weight_grad = rows_product(active, grad_two).astype(jnp.bfloat16)
    contract_bias_grad = jnp.sum(grad_two, axis=0, dtype=jnp.float32)
    grad_before = pull_active(transposed_product(grad_two, contract_weight))[0].astype(jnp.bfloat16)
    expand_weight_grad = rows_product(middle, grad_before).astype(jnp.bfloat16)
    expand_bias_grad = jnp.sum(grad_before, axis=0, dtype=jnp.float32)
    grad_middle = summed(
        lambda rows: transposed_product(rows, expand_weight),
        (grad_before[:own_rows], grad_before[own_rows:]),
    )
    branch_two = summed(
        lambda rows: jnp.dot(rows, contract_weight, preferred_element_type=jnp.float32),
        (active[:own_rows], active[own_rows:]),
    ) + contract_bias.astype(jnp.float32)
    result = (hidden + live * branch_two).astype(jnp.bfloat16)
    grad_norm_two, gain_second_grad, shift_second_grad = pull_second(grad_middle)
    grad_hidden = upstream + grad_norm_two
    own_branch = (live * grad_hidden).astype(jnp.bfloat16)
    grad_branch = in_order(own_branch, swap(own_branch))
    output_weight_grad = rows_product(grad_branch, mixed)
    output_bias_grad = jnp.sum(grad_branch, axis=0, dtype=jnp.float32)
    grad_mixed = transposed_product(grad_branch, output_weight).astype(jnp.bfloat16)
    grad_query, grad_keys, grad_values = attention_call(
        backward_kernel, (jnp.bfloat16,) * 3, 2, 6 * pairs, "attend_back",
        firsts, query, keys, values, logs, grad_mixed,
    )
    query_weight_grad = rows_product(normed, grad_query)
    key_weight_grad = rows_product(normed, grad_keys)
    value_weight_grad = rows_product(normed, grad_values)
    query_bias_grad = jnp.sum(grad_query, axis=0, dtype=jnp.float32)
    value_bias_grad = jnp.sum(grad_values, axis=0, dtype=jnp.float32)
    query_rows, keys_rows, values_rows = halves(grad_query), halves(grad_keys), halves(grad_values)
    grad_normed = summed(
        lambda rows: transposed_product(rows[0], query_weight)
        + transposed_product(rows[1], key_weight)
        + transposed_product(rows[2], value_weight),
        tuple(zip(query_rows, keys_rows, values_rows)),
    )
    grad_norm_one, gain_first_grad, shift_first_grad = pull_first(grad_normed)
    tokens_grad = (grad_hidden + grad_norm_one).astype(jnp.bfloat16)
    norms = jnp.stack([gain_first_grad, shift_first_grad, gain_second_grad, shift_second_grad])
    norms = norms + swap(norms)
    small = (
        norms, query_bias_grad, value_bias_grad, output_bias_grad, expand_bias_grad,
        contract_bias_grad,
    )
    small = jnp.concatenate([item.reshape(-1, width) for item in small], axis=0)
    small_rows = small.shape[0]
    small = jnp.pad(small, ((0, -small_rows % 256), (0, 0)))
    depth = query_weight.shape[0]
    packed = jnp.concatenate([value_weight_grad, small], axis=0).astype(jnp.bfloat16)
    (
        contract_weight_grad,
        expand_weight_grad,
        output_weight_grad,
        query_weight_grad,
        key_weight_grad,
        packed,
    ) = sum_over_groups(
        (
            contract_weight_grad,
            expand_weight_grad,
            output_weight_grad.astype(jnp.bfloat16),
            query_weight_grad.astype(jnp.bfloat16),
            key_weight_grad.astype(jnp.bfloat16),
            packed,
        ),
        lax.axis_size("dp"),
    )
    packed = packed.astype(jnp.float32)
    value_weight_grad = packed[:depth]
    small = packed[depth : depth + small_rows].reshape(-1)
    features = gain_first.shape[0]
    sizes = (features,) * 4 + (width, width, features, expand_bias.shape[0], features)
    cuts, at = [], 0
    for size in sizes:
        cuts.append(small[at : at + size])
        at += size
    gain_first_grad, shift_first_grad, gain_second_grad, shift_second_grad = cuts[:4]
    query_bias_grad, value_bias_grad, output_bias_grad = cuts[4:7]
    expand_bias_grad, contract_bias_grad = cuts[7:]
    key_weight_grad = key_weight_grad.astype(jnp.float32)
    query_weight_grad = query_weight_grad.astype(jnp.float32)
    output_weight_grad = output_weight_grad.astype(jnp.float32).T
    expand_weight_grad = expand_weight_grad.astype(jnp.float32)
    contract_weight_grad = contract_weight_grad.astype(jnp.float32)
    return (
        result,
        tokens_grad,
        gain_first_grad,
        shift_first_grad,
        query_weight_grad,
        key_weight_grad,
        value_weight_grad,
        query_bias_grad,
        value_bias_grad,
        output_weight_grad,
        output_bias_grad,
        gain_second_grad,
        shift_second_grad,
        expand_weight_grad,
        expand_bias_grad,
        contract_weight_grad,
        contract_bias_grad,
    )


def solution(mesh):
    in_specs = (
        P(("dp", "tensor"), None),
        P(),
        P(),
        P(),
        P(),
        P(None, "tensor"),
        P(None, "tensor"),
        P(None, "tensor"),
        P("tensor"),
        P("tensor"),
        P("tensor", None),
        P(),
        P(),
        P(),
        P(None, "tensor"),
        P("tensor"),
        P("tensor", None),
        P(),
        P(("dp", "tensor"), None),
    )
    out_specs = (
        P(("dp", "tensor"), None),
        P(("dp", "tensor"), None),
        P(),
        P(),
        P(None, "tensor"),
        P(None, "tensor"),
        P(None, "tensor"),
        P("tensor"),
        P("tensor"),
        P("tensor", None),
        P(),
        P(),
        P(),
        P(None, "tensor"),
        P("tensor"),
        P("tensor", None),
        P(),
    )
    return jax.shard_map(
        on_device, mesh=mesh, in_specs=in_specs, out_specs=out_specs, check_vma=False
    )
```

```python
import functools

import jax
import jax.numpy as jnp
from jax import lax
from jax.experimental import pallas as pl
from jax.experimental.pallas import tpu as pltpu
from jax.sharding import PartitionSpec as P

HD = 64


epsilon = 1e-05


def layer_norm(values, gain, shift):
    average = jnp.mean(values, axis=-1, keepdims=True)
    centred = values - average
    variance = jnp.mean(centred * centred, axis=-1, keepdims=True)
    return centred * lax.rsqrt(variance + epsilon) * gain + shift


def gelu_tanh(values):
    return jax.nn.gelu(values, approximate=True)


def row_segments(lengths, owners, group, total_rows):
    count = lengths.shape[0]
    index = jnp.arange(count, dtype=jnp.int32)
    same = owners[None, :] == owners[:, None]
    earlier = index[None, :] < index[:, None]
    starts = jnp.sum(jnp.where(same & earlier, lengths[None, :], 0), axis=1, dtype=jnp.int32)
    positions = jnp.arange(total_rows, dtype=jnp.int32)[:, None]
    inside = (
        (owners[None, :] == group)
        & (positions >= starts[None, :])
        & (positions < starts[None, :] + lengths[None, :])
    )
    segments = jnp.sum(jnp.where(inside, index[None, :] + 1, 0), axis=1, dtype=jnp.int32)
    used = jnp.sum(jnp.where(owners == group, lengths, 0), dtype=jnp.int32)
    first = jnp.sum(jnp.where(inside, starts[None, :], 0), axis=1, dtype=jnp.int32)
    return segments, jnp.where(segments > 0, first, used)


def rows_product(left, right):
    return lax.dot_general(
        left, right, (((0,), (0,)), ((), ())), preferred_element_type=jnp.float32
    )


def transposed_product(left, right):
    return lax.dot_general(
        left, right, (((1,), (1,)), ((), ())), preferred_element_type=jnp.float32
    )


QB = 256
MASKED = -1e30


def heads_dot(left, right, left_dim, right_dim):
    return lax.dot_general(
        left, right, (((left_dim,), (right_dim,)), ((), ())), preferred_element_type=jnp.float32
    )


def fill_mask(first_ref, mask_ref):
    total = mask_ref.shape[0]
    for start in range(0, total, QB):
        rows = start + lax.broadcasted_iota(jnp.int32, (QB, total), 0)
        columns = lax.broadcasted_iota(jnp.int32, (QB, total), 1)
        allowed = (columns >= first_ref[start : start + QB, :]) & (columns <= rows)
        mask_ref[start : start + QB, :] = jnp.where(allowed, 0.0, MASKED)


def forward_kernel(first_ref, query_ref, keys_ref, values_ref, mixed_ref, log_ref, mask_ref):
    @pl.when(pl.program_id(0) == 0)
    def _():
        fill_mask(first_ref, mask_ref)

    total = query_ref.shape[0]
    for start in range(0, total, QB):
        stop = start + QB
        outs, logs = [], []
        for h in range(2):
            lanes = slice(h * HD, (h + 1) * HD)
            scores = heads_dot(query_ref[start:stop, lanes], keys_ref[:stop, lanes], 1, 1)
            scores = scores + mask_ref[start:stop, :stop]
            top = jnp.max(scores, axis=-1, keepdims=True)
            powers = jnp.exp(scores - top)
            sums = jnp.sum(powers, axis=-1, keepdims=True)
            probs = (powers * (1.0 / sums)).astype(jnp.bfloat16)
            outs.append(heads_dot(probs, values_ref[:stop, lanes], 1, 0))
            logs.append(jnp.broadcast_to(top + jnp.log(sums), (QB, HD)))
        mixed_ref[start:stop, :] = jnp.concatenate(outs, axis=1).astype(jnp.bfloat16)
        log_ref[start:stop, :] = jnp.concatenate(logs, axis=1)


def backward_kernel(
    first_ref, query_ref, keys_ref, values_ref, log_ref, grad_ref,
    grad_query_ref, grad_keys_ref, grad_values_ref, mask_ref, keys_sum, values_sum,
):
    @pl.when(pl.program_id(0) == 0)
    def _():
        fill_mask(first_ref, mask_ref)

    total = query_ref.shape[0]
    for start in range(total - QB, -1, -QB):
        stop = start + QB
        parts = ([], [], [])
        for h in range(2):
            lanes = slice(h * HD, (h + 1) * HD)
            query = query_ref[start:stop, lanes]
            grad = grad_ref[start:stop, lanes]
            keys = keys_ref[:stop, lanes]
            scores = heads_dot(query, keys, 1, 1) + mask_ref[start:stop, :stop]
            probs = jnp.exp(scores - log_ref[start:stop, h * HD : h * HD + 1])
            grad_probs = heads_dot(grad, values_ref[:stop, lanes], 1, 1)
            inner = jnp.sum(probs * grad_probs, axis=-1, keepdims=True)
            grad_scores = (probs * (grad_probs - inner)).astype(jnp.bfloat16)
            parts[0].append(heads_dot(grad_scores, keys, 1, 0))
            parts[1].append(heads_dot(grad_scores, query, 0, 0))
            parts[2].append(heads_dot(probs.astype(jnp.bfloat16), grad, 0, 0))
        grad_query_ref[start:stop, :] = (
            jnp.concatenate(parts[0], axis=1) * (HD ** (-0.5))
        ).astype(jnp.bfloat16)
        for sums, part in ((keys_sum, parts[1]), (values_sum, parts[2])):
            part = jnp.concatenate(part, axis=1)
            if stop == total:
                sums[...] = part
            else:
                sums[:stop, :] += part
    grad_keys_ref[...] = keys_sum[...].astype(jnp.bfloat16)
    grad_values_ref[...] = values_sum[...].astype(jnp.bfloat16)


def attention_call(kernel, out_types, scratch, flops, name, first, *operands):
    rows, width = operands[0].shape
    pair = pl.BlockSpec((rows, 2 * HD), lambda i: (0, i))
    return pl.pallas_call(
        kernel,
        grid=(width // (2 * HD),),
        in_specs=[pl.BlockSpec((rows, 1), lambda i: (0, 0))] + [pair] * len(operands),
        out_specs=[pair] * len(out_types),
        out_shape=[jax.ShapeDtypeStruct((rows, width), kind) for kind in out_types],
        scratch_shapes=[pltpu.VMEM((rows, rows), jnp.float32)]
        + [pltpu.VMEM((rows, 2 * HD), jnp.float32)] * scratch,
        compiler_params=pltpu.CompilerParams(vmem_limit_bytes=40 * 1024 * 1024),
        cost_estimate=pl.CostEstimate(
            flops=flops, bytes_accessed=8 * rows * width * 2, transcendentals=rows * rows * 4
        ),
        name=name,
    )(first, *operands)


def swap(values):
    return lax.ppermute(values, "tensor", [(0, 1), (1, 0)])


def sum_kernel(groups, orders, chains, count, *refs):
    inputs, outputs = refs[:count], refs[count : 2 * count]
    works, arrived = refs[2 * count : 3 * count], refs[3 * count : 4 * count]
    send_sem, recv_sem = refs[4 * count :]
    group = lax.axis_index("dp")
    steps = len(orders[0])
    digit = [(group // (1 << bit)) % 2 for bit in range(steps)]
    partner = [group + (1 - 2 * digit[bit]) * (1 << bit) for bit in range(steps)]

    barrier = pltpu.get_barrier_semaphore()
    for bit in range(steps):
        pl.semaphore_signal(
            barrier, inc=1, device_id={"dp": partner[bit]}, device_id_type=pl.DeviceIdType.MESH
        )
    pl.semaphore_wait(barrier, steps)

    def copy(chain, step, bit, source, target):
        slot = chain * 2 * steps + step
        made = pltpu.make_async_remote_copy(
            src_ref=source,
            dst_ref=target,
            send_sem=send_sem.at[slot],
            recv_sem=recv_sem.at[slot],
            device_id={"dp": partner[bit]},
            device_id_type=pl.DeviceIdType.MESH,
        )
        made.start()
        return made

    def rows_at(start, size):
        return pl.ds(pl.multiple_of(start, 16), size)

    offsets = [[0] for _ in chains]
    pending = [None for _ in chains]
    started = []

    def scatter_start(c, step):
        array, low, high, kind = chains[c]
        rows = inputs[array].shape[0]
        half = rows >> (step + 1)
        bit = orders[kind][step]
        source = inputs[array] if step == 0 else works[array]
        sent = offsets[c][-1] + (1 - digit[bit]) * half
        pending[c] = copy(
            c, step, bit,
            source.at[rows_at(sent, half), low:high],
            arrived[array].at[rows - 2 * half : rows - half, low:high],
        )
        started.append(pending[c])
        offsets[c].append(offsets[c][-1] + digit[bit] * half)

    def scatter_add(c, step):
        array, low, high, kind = chains[c]
        rows = inputs[array].shape[0]
        half = rows >> (step + 1)
        kept = offsets[c][-1]
        pending[c].wait_recv()
        tile = 48 if half % 48 == 0 else 16
        source = inputs[array] if step == 0 else works[array]
        target = outputs[array] if step == steps - 1 else works[array]

        def add(i, carry):
            here = rows_at(kept + i * tile, tile)
            there = rows_at(rows - 2 * half + i * tile, tile)
            total = source[here, low:high].astype(jnp.float32) + arrived[array][
                there, low:high
            ].astype(jnp.float32)
            target[here, low:high] = total.astype(jnp.bfloat16)
            return carry

        lax.fori_loop(0, half // tile, add, 0)

    def gather_start(c, step):
        array, low, high, kind = chains[c]
        size = inputs[array].shape[0] >> step
        block = outputs[array].at[rows_at(offsets[c][step], size), low:high]
        pending[c] = copy(c, 2 * steps - step, orders[kind][step - 1], block, block)
        started.append(pending[c])

    every = range(len(chains))
    for c in every:
        scatter_start(c, 0)
    for step in range(steps):
        for c in every:
            scatter_add(c, step)
            if step < steps - 1:
                scatter_start(c, step + 1)
            else:
                gather_start(c, steps)
    for step in range(steps - 1, 0, -1):
        for c in every:
            pending[c].wait_recv()
            gather_start(c, step)
    for c in every:
        pending[c].wait_recv()
    for made in started:
        made.wait_send()


def sum_over_groups(arrays, groups):
    if any(array.shape[0] % (16 * groups) for array in arrays):
        return lax.psum(tuple(arrays), "dp")
    bits = list(range(groups.bit_length() - 1))
    orders = (bits, bits[1:2] + bits[:1] + bits[2:], bits[2:] + bits[:2])
    chains = []
    for index, array in enumerate(arrays):
        width = array.shape[1]
        if index == 0:
            cuts = [(0, width // 2, 0), (width // 2, width, 1)]
        elif index in (1, 2):
            third = width // 3
            cuts = [(i * third, (i + 1) * third, i) for i in range(3)]
        else:
            cuts = [(0, width, index - 3)]
        chains += [(index,) + cut for cut in cuts]
    chains.sort(key=lambda chain: (chain[0] > 1, chain[3] != 2))
    count = len(arrays)
    slots = len(chains) * 2 * len(bits)
    shapes = [jax.ShapeDtypeStruct(array.shape, array.dtype) for array in arrays]
    buffers = [pltpu.VMEM(array.shape, array.dtype) for array in arrays]
    vmem = pl.BlockSpec(memory_space=pltpu.VMEM)
    return pl.pallas_call(
        functools.partial(sum_kernel, groups, orders, chains, count),
        out_shape=shapes,
        in_specs=[vmem] * count,
        out_specs=[vmem] * count,
        scratch_shapes=buffers
        + buffers
        + [pltpu.SemaphoreType.DMA((slots,)), pltpu.SemaphoreType.DMA((slots,))],
        compiler_params=pltpu.CompilerParams(
            collective_id=0, has_side_effects=True, vmem_limit_bytes=48 * 1024 * 1024
        ),
        name="sum_over_groups",
    )(*arrays)


def on_device(
    tokens,
    lengths,
    owners,
    gain_first,
    shift_first,
    query_weight,
    key_weight,
    value_weight,
    query_bias,
    value_bias,
    output_weight,
    output_bias,
    gain_second,
    shift_second,
    expand_weight,
    expand_bias,
    contract_weight,
    contract_bias,
    cotangent,
):
    own_rows = tokens.shape[0]
    group = lax.axis_index("dp")
    side = lax.axis_index("tensor")
    first_row = side * own_rows
    other_row = (1 - side) * own_rows

    def in_order(own, other):
        return jnp.concatenate(
            [jnp.where(side == 0, own, other), jnp.where(side == 0, other, own)], axis=0
        )

    def halves(values):
        return (
            lax.dynamic_slice_in_dim(values, first_row, own_rows, 0),
            lax.dynamic_slice_in_dim(values, other_row, own_rows, 0),
        )

    segments, firsts = row_segments(lengths, owners, group, 2 * own_rows)
    firsts = firsts[:, None]
    own_segments = lax.dynamic_slice_in_dim(segments, first_row, own_rows, 0)
    live = (own_segments > 0).astype(jnp.float32)[:, None]
    scale = HD ** (-0.5)
    width = query_weight.shape[1]
    upstream = cotangent.astype(jnp.float32)
    own_two = (live * upstream).astype(jnp.bfloat16)
    inputs = tokens.astype(jnp.float32)
    normed_value, pull_first = jax.vjp(
        layer_norm, inputs, gain_first.astype(jnp.float32), shift_first.astype(jnp.float32)
    )
    own_normed = normed_value.astype(jnp.bfloat16)
    normed = in_order(own_normed, swap(own_normed))
    grad_two = jnp.concatenate([own_two, swap(own_two)], axis=0)
    query = (
        jnp.dot(normed, query_weight, preferred_element_type=jnp.float32)
        + query_bias.astype(jnp.float32)
    ).astype(jnp.bfloat16) * jnp.bfloat16(scale)
    keys = jnp.dot(normed, key_weight, preferred_element_type=jnp.float32).astype(jnp.bfloat16)
    values = (
        jnp.dot(normed, value_weight, preferred_element_type=jnp.float32)
        + value_bias.astype(jnp.float32)
    ).astype(jnp.bfloat16)
    pairs = 2 * own_rows * 2 * own_rows * width
    mixed, logs = attention_call(
        forward_kernel, (jnp.bfloat16, jnp.float32), 0, 3 * pairs, "attend",
        firsts, query, keys, values,
    )

    def summed(product, values, send_type=jnp.bfloat16):
        own, other = values
        received = swap(product(other).astype(send_type))
        return product(own) + received.astype(jnp.float32)

    branch = summed(
        lambda rows: jnp.dot(rows, output_weight, preferred_element_type=jnp.float32),
        halves(mixed),
    ) + output_bias.astype(jnp.float32)
    hidden = inputs + live * branch
    middle_value, pull_second = jax.vjp(
        layer_norm, hidden, gain_second.astype(jnp.float32), shift_second.astype(jnp.float32)
    )
    own_middle = middle_value.astype(jnp.bfloat16)
    middle = jnp.concatenate([own_middle, swap(own_middle)], axis=0)
    before = jnp.dot(
        middle, expand_weight, preferred_element_type=jnp.float32
    ) + expand_bias.astype(jnp.float32)
    active_value, pull_active = jax.vjp(gelu_tanh, before)
    active = active_value.astype(jnp.bfloat16)
    contract_weight_grad = rows_product(active, grad_two).astype(jnp.bfloat16)
    contract_bias_grad = jnp.sum(grad_two, axis=0, dtype=jnp.float32)
    grad_before = pull_active(transposed_product(grad_two, contract_weight))[0].astype(jnp.bfloat16)
    expand_weight_grad = rows_product(middle, grad_before).astype(jnp.bfloat16)
    expand_bias_grad = jnp.sum(grad_before, axis=0, dtype=jnp.float32)
    grad_middle = summed(
        lambda rows: transposed_product(rows, expand_weight),
        (grad_before[:own_rows], grad_before[own_rows:]),
    )
    branch_two = summed(
        lambda rows: jnp.dot(rows, contract_weight, preferred_element_type=jnp.float32),
        (active[:own_rows], active[own_rows:]),
    ) + contract_bias.astype(jnp.float32)
    result = (hidden + live * branch_two).astype(jnp.bfloat16)
    grad_norm_two, gain_second_grad, shift_second_grad = pull_second(grad_middle)
    grad_hidden = upstream + grad_norm_two
    own_branch = (live * grad_hidden).astype(jnp.bfloat16)
    grad_branch = in_order(own_branch, swap(own_branch))
    output_weight_grad = rows_product(grad_branch, mixed)
    output_bias_grad = jnp.sum(grad_branch, axis=0, dtype=jnp.float32)
    grad_mixed = transposed_product(grad_branch, output_weight).astype(jnp.bfloat16)
    grad_query, grad_keys, grad_values = attention_call(
        backward_kernel, (jnp.bfloat16,) * 3, 2, 6 * pairs, "attend_back",
        firsts, query, keys, values, logs, grad_mixed,
    )
    query_weight_grad = rows_product(normed, grad_query)
    key_weight_grad = rows_product(normed, grad_keys)
    value_weight_grad = rows_product(normed, grad_values)
    query_bias_grad = jnp.sum(grad_query, axis=0, dtype=jnp.float32)
    value_bias_grad = jnp.sum(grad_values, axis=0, dtype=jnp.float32)
    query_rows, keys_rows, values_rows = halves(grad_query), halves(grad_keys), halves(grad_values)
    grad_normed = summed(
        lambda rows: transposed_product(rows[0], query_weight)
        + transposed_product(rows[1], key_weight)
        + transposed_product(rows[2], value_weight),
        tuple(zip(query_rows, keys_rows, values_rows)),
    )
    grad_norm_one, gain_first_grad, shift_first_grad = pull_first(grad_normed)
    tokens_grad = (grad_hidden + grad_norm_one).astype(jnp.bfloat16)
    norms = jnp.stack([gain_first_grad, shift_first_grad, gain_second_grad, shift_second_grad])
    norms = norms + swap(norms)
    small = (
        norms, query_bias_grad, value_bias_grad, output_bias_grad, expand_bias_grad,
        contract_bias_grad,
    )
    small = jnp.concatenate([item.reshape(-1, width) for item in small], axis=0)
    small_rows = small.shape[0]
    small = jnp.pad(small, ((0, -small_rows % 256), (0, 0)))
    depth = query_weight.shape[0]
    packed = jnp.concatenate([value_weight_grad, small], axis=0).astype(jnp.bfloat16)
    (
        contract_weight_grad,
        expand_weight_grad,
        output_weight_grad,
        query_weight_grad,
        key_weight_grad,
        packed,
    ) = sum_over_groups(
        (
            contract_weight_grad,
            expand_weight_grad,
            output_weight_grad.astype(jnp.bfloat16),
            query_weight_grad.astype(jnp.bfloat16),
            key_weight_grad.astype(jnp.bfloat16),
            packed,
        ),
        lax.axis_size("dp"),
    )
    packed = packed.astype(jnp.float32)
    value_weight_grad = packed[:depth]
    small = packed[depth : depth + small_rows].reshape(-1)
    features = gain_first.shape[0]
    sizes = (features,) * 4 + (width, width, features, expand_bias.shape[0], features)
    cuts, at = [], 0
    for size in sizes:
        cuts.append(small[at : at + size])
        at += size
    gain_first_grad, shift_first_grad, gain_second_grad, shift_second_grad = cuts[:4]
    query_bias_grad, value_bias_grad, output_bias_grad = cuts[4:7]
    expand_bias_grad, contract_bias_grad = cuts[7:]
    key_weight_grad = key_weight_grad.astype(jnp.float32)
    query_weight_grad = query_weight_grad.astype(jnp.float32)
    output_weight_grad = output_weight_grad.astype(jnp.float32).T
    expand_weight_grad = expand_weight_grad.astype(jnp.float32)
    contract_weight_grad = contract_weight_grad.astype(jnp.float32)
    return (
        result,
        tokens_grad,
        gain_first_grad,
        shift_first_grad,
        query_weight_grad,
        key_weight_grad,
        value_weight_grad,
        query_bias_grad,
        value_bias_grad,
        output_weight_grad,
        output_bias_grad,
        gain_second_grad,
        shift_second_grad,
        expand_weight_grad,
        expand_bias_grad,
        contract_weight_grad,
        contract_bias_grad,
    )


def solution(mesh):
    in_specs = (
        P(("dp", "tensor"), None),
        P(),
        P(),
        P(),
        P(),
        P(None, "tensor"),
        P(None, "tensor"),
        P(None, "tensor"),
        P("tensor"),
        P("tensor"),
        P("tensor", None),
        P(),
        P(),
        P(),
        P(None, "tensor"),
        P("tensor"),
        P("tensor", None),
        P(),
        P(("dp", "tensor"), None),
    )
    out_specs = (
        P(("dp", "tensor"), None),
        P(("dp", "tensor"), None),
        P(),
        P(),
        P(None, "tensor"),
        P(None, "tensor"),
        P(None, "tensor"),
        P("tensor"),
        P("tensor"),
        P("tensor", None),
        P(),
        P(),
        P(),
        P(None, "tensor"),
        P("tensor"),
        P("tensor", None),
        P(),
    )
    return jax.shard_map(
        on_device, mesh=mesh, in_specs=in_specs, out_specs=out_specs, check_vma=False
    )
```
